1024 devices in a mesh: nodes: 64 (over x, z), hidden: 16 (over y, core).
Axes of the slice: x: 4, y: 8, z: 16, core: 2. Of those that a mesh axis runs over, the one named last changes fastest.
Arguments:
- fine_nodes: bfloat16 [131072, 256], P(('nodes', 'hidden')), may hold values from -6 to 6
- fine_edges: bfloat16 [131072, 6, 256], P(('nodes', 'hidden')), may hold values from -6 to 6
- fine_neighbours: int32 [131072, 6], P(('nodes', 'hidden')), may hold values from -1 to 383, as said below
- group_send: int32 [64, 16, 16, 8], P('nodes'), may hold values from 0 to 127
- halo_send: int32 [1024, 64, 2], P(('nodes', 'hidden')), may hold values from 0 to 127
- pool_send: int32 [1024, 64, 4], P(('nodes', 'hidden')), may hold values from -1 to 127, as said below
- pool_recv: int32 [1024, 64, 4], P(('nodes', 'hidden')), may hold values from -1 to 15, as said below
- coarse_neighbours: int32 [16384, 6], P(('nodes', 'hidden')), may hold values from -1 to 15, as said below
- edge_in: bfloat16 [768, 1024], replicated, may hold values from -0.21875 to 0.21875
- edge_out: bfloat16 [1024, 256], replicated, may hold values from -0.1875 to 0.1875
- node_in: bfloat16 [512, 1024], replicated, may hold values from -0.25 to 0.25
- node_out: bfloat16 [1024, 256], replicated, may hold values from -0.1875 to 0.1875
- coarse_edge_in: bfloat16 [512, 1024], replicated, may hold values from -0.25 to 0.25
- coarse_edge_out: bfloat16 [1024, 256], replicated, may hold values from -0.1875 to 0.1875
- coarse_node_in: bfloat16 [512, 1024], replicated, may hold values from -0.25 to 0.25
- coarse_node_out: bfloat16 [1024, 256], replicated, may hold values from -0.1875 to 0.1875
Outputs:
- fine_result: bfloat16 [131072, 256], P(('nodes', 'hidden'))
- edge_result: bfloat16 [131072, 6, 256], P(('nodes', 'hidden'))
- coarse_result: bfloat16 [16384, 256], P(('nodes', 'hidden'))
The draws below stay inside these ranges and needn't reach their ends.
Inputs may be any that keep to these rules, and one draw needn't show every extreme that they name: `fine_neighbours`: -1 marks an empty slot; empty slots are the last ones of a node and at least four slots of every node are filled; every value of 128 or more that a device can receive is named by some slot of that device's nodes. `pool_send`: rows q of the sending device's 128 fine nodes, or -1; each of those rows appears exactly once in the device's lists, and filled slots of one peer come first; for each index along hidden, one device along nodes gets all 4 slots filled from every sender. `pool_recv`: at device (m, h), entry [g, s] is the coarse node, among the device's 16, of the row that device (g, h) puts in pool_send slot [m, s]; -1 exactly where that slot is -1; on every device some coarse node has no member. `coarse_neighbours`: indices among the 16 coarse nodes of the same device; -1 marks an empty slot; empty slots are the last ones and at least three are filled.
All inputs are finite; a program needn't handle non-finite values.
Results may differ from the reference program's by a relative error of at most 0.015.
Values may be sent and summed in bfloat16 or wider, within the bound.
A program may use at most 64 MiB of HBM per device.

```python
import jax
import jax.numpy as jnp
from jax import lax

L = 256
HID = 1024
NS = 128
DEG = 6
SLOT_H = 8
SLOT = 2
NC_DEV = 16
DEG_C = 6
CAP = 4
NF = 131072
NC = 16384
N_NODES = 64
N_HIDDEN = 16


def pool_lists(key):
    key = jax.random.fold_in(key, 71)
    keys = jax.random.split(key, 6)
    devices_all = N_NODES * N_HIDDEN
    slot_total = N_NODES * CAP
    full_peer = jax.random.randint(keys[0], (1, N_HIDDEN, 1, 1), 0, N_NODES)
    base = jax.random.randint(keys[1], (N_NODES, N_HIDDEN, N_NODES, CAP), 0, 1 << 16)
    peer_ids = jnp.arange(N_NODES, dtype=jnp.int32)[None, None, :, None]
    penalty = jnp.where(peer_ids == full_peer, 0, 1 << 16)
    scores = (base + penalty).reshape(devices_all, slot_total) * slot_total + jnp.arange(slot_total, dtype=jnp.int32)[None, :]
    order = jnp.argsort(scores, axis=1)
    rank = jnp.argsort(order, axis=1).astype(jnp.int32)
    filled = (rank < NS).reshape(devices_all, N_NODES, CAP)
    counts = jnp.sum(filled.astype(jnp.int32), axis=2)
    offsets = jnp.cumsum(counts, axis=1) - counts
    slot_ids = jnp.arange(CAP, dtype=jnp.int32)[None, None, :]
    live = slot_ids < counts[:, :, None]
    position = jnp.where(live, offsets[:, :, None] + slot_ids, 0).astype(jnp.int32)
    row_scores = jax.random.randint(keys[2], (devices_all, NS), 0, 1 << 16) * NS + jnp.arange(NS, dtype=jnp.int32)[None, :]
    row_perm = jnp.argsort(row_scores, axis=1).astype(jnp.int32)
    rows = jnp.take_along_axis(row_perm, position.reshape(devices_all, -1), axis=1).reshape(devices_all, N_NODES, CAP)
    send_lists = jnp.where(live, rows, -1).astype(jnp.int32)
    send_turned = jnp.transpose(send_lists.reshape(N_NODES, N_HIDDEN, N_NODES, CAP), (2, 1, 0, 3))
    excluded = jax.random.randint(keys[3], (N_NODES, N_HIDDEN, 1, 1), 0, NC_DEV)
    first_pick = jax.random.randint(keys[4], send_turned.shape, 0, NC_DEV - 1)
    second_pick = jax.random.randint(keys[5], send_turned.shape, 0, NC_DEV - 1)
    cluster_ids = jnp.minimum(first_pick, second_pick)
    cluster_ids = cluster_ids + (cluster_ids >= excluded).astype(jnp.int32)
    recv_lists = jnp.where(send_turned >= 0, cluster_ids, -1).reshape(devices_all, N_NODES, CAP).astype(jnp.int32)
    return (send_lists, recv_lists)


def draw_pool_send(key, part):
    send_lists, recv_lists = pool_lists(key)
    return send_lists


def draw_pool_recv(key, part):
    send_lists, recv_lists = pool_lists(key)
    return recv_lists


def draw_fine_neighbours(key, part):
    key = jax.random.fold_in(key, 11)
    keys = jax.random.split(key, 5)
    devices_all = N_NODES * N_HIDDEN
    received = N_HIDDEN * SLOT_H + N_NODES * SLOT
    degree = jax.random.randint(keys[0], (devices_all, NS, 1), 4, DEG + 1)
    slot_index = jnp.arange(DEG, dtype=jnp.int32)[None, None, :]
    own_pick = jax.random.randint(keys[1], (devices_all, NS, DEG), 0, NS)
    far_pick = NS + jax.random.randint(keys[2], (devices_all, NS, DEG), 0, received)
    chooser = jax.random.randint(keys[3], (devices_all, NS, DEG), 0, 2)
    picked = jnp.where(chooser == 0, own_pick, far_pick)
    scores = jax.random.randint(keys[4], (devices_all, NS * 4), 0, 1 << 16) * (NS * 4) + jnp.arange(NS * 4, dtype=jnp.int32)[None, :]
    order = jnp.argsort(scores, axis=1)
    rank = jnp.argsort(order, axis=1).astype(jnp.int32).reshape(devices_all, NS, 4)
    first = jnp.where(rank < received, NS + rank, picked[:, :, :4])
    picked = jnp.concatenate([first, picked[:, :, 4:]], axis=2)
    return jnp.where(slot_index < degree, picked, -1).reshape(NF, DEG).astype(jnp.int32)


def draw_coarse_neighbours(key, part):
    key = jax.random.fold_in(key, 23)
    keys = jax.random.split(key, 2)
    total_rows = NC_DEV * N_NODES * N_HIDDEN
    degree = jax.random.randint(keys[0], (total_rows, 1), 3, DEG_C + 1)
    slot_index = jnp.arange(DEG_C, dtype=jnp.int32)[None, :]
    picked = jax.random.randint(keys[1], (total_rows, DEG_C), 0, NC_DEV)
    return jnp.where(slot_index < degree, picked, -1).astype(jnp.int32)


def with_ends(array, own_key, least, largest):
    longest = array.shape.index(max(array.shape))
    spots = []
    for shift in (0, 1):
        where = [jax.random.randint(jax.random.fold_in(own_key, axis), (), 0, length) for axis, length in enumerate(array.shape)]
        where[longest] = (where[longest] + shift) % array.shape[longest]
        spots.append(tuple(where))
    return array.at[spots[0]].set(least).at[spots[1]].set(largest)


def block_scale(own_key, dims, cuts, low, top_value):
    level = 1.0
    for dim, shards_of in cuts:
        draws = jax.random.uniform(jax.random.fold_in(jax.random.fold_in(own_key, 6), dim), (shards_of,), jnp.float32, low / len(cuts), top_value / len(cuts))
        level = level * jnp.repeat(jnp.exp(draws), dims[dim] // shards_of).reshape((-1,) + (1,) * (len(dims) - 1 - dim))
    return level


def normal_values(stream_key, dims, deviation, bound, shards=(), kind=jnp.bfloat16):
    level = block_scale(stream_key, dims, shards, -0.22, 0.18) if shards else 1.0
    drawn = jax.random.normal(stream_key, dims, jnp.float32) * deviation * level
    return jnp.minimum(jnp.maximum(drawn, -bound), bound).astype(kind)


def setup_inputs(seed: int = 0) -> dict:
    key_list = jax.random.split(jax.random.key(seed), 17)
    fine_nodes = normal_values(key_list[0], (NF, L), 1.0, 6.0, ((0, 1024),))
    fine_edges = normal_values(key_list[1], (NF, DEG, L), 1.0, 6.0, ((0, 1024),))
    fine_neighbours = draw_fine_neighbours(jax.random.fold_in(key_list[16], 71), 0)
    group_send = with_ends(jax.random.randint(key_list[3], (N_NODES, N_HIDDEN, N_HIDDEN, SLOT_H), 0, NS), jax.random.fold_in(key_list[3], 1), 0, NS - 1).astype(jnp.int32)
    halo_send = with_ends(jax.random.randint(key_list[4], (N_NODES * N_HIDDEN, N_NODES, SLOT), 0, NS), jax.random.fold_in(key_list[4], 1), 0, NS - 1).astype(jnp.int32)
    pool_send = draw_pool_send(jax.random.fold_in(key_list[16], 71), 0)
    pool_recv = draw_pool_recv(jax.random.fold_in(key_list[16], 71), 0)
    coarse_neighbours = draw_coarse_neighbours(jax.random.fold_in(key_list[16], 71), 0)
    edge_in = normal_values(key_list[8], (3 * L, HID), (3 * L) ** -0.5, 0.21875)
    edge_out = normal_values(key_list[9], (HID, L), HID ** -0.5, 0.1875)
    node_in = normal_values(key_list[10], (2 * L, HID), (2 * L) ** -0.5, 0.25)
    node_out = normal_values(key_list[11], (HID, L), HID ** -0.5, 0.1875)
    coarse_edge_in = normal_values(key_list[12], (2 * L, HID), (2 * L) ** -0.5, 0.25)
    coarse_edge_out = normal_values(key_list[13], (HID, L), HID ** -0.5, 0.1875)
    coarse_node_in = normal_values(key_list[14], (2 * L, HID), (2 * L) ** -0.5, 0.25)
    coarse_node_out = normal_values(key_list[15], (HID, L), HID ** -0.5, 0.1875)
    return {"fine_nodes": fine_nodes, "fine_edges": fine_edges, "fine_neighbours": fine_neighbours, "group_send": group_send, "halo_send": halo_send, "pool_send": pool_send, "pool_recv": pool_recv, "coarse_neighbours": coarse_neighbours, "edge_in": edge_in, "edge_out": edge_out, "node_in": node_in, "node_out": node_out, "coarse_edge_in": coarse_edge_in, "coarse_edge_out": coarse_edge_out, "coarse_node_in": coarse_node_in, "coarse_node_out": coarse_node_out}


EPSILON = 1e-05

def layer_norm(values):
    average = lax.optimization_barrier(jnp.mean(values, axis=-1, keepdims=True))
    centred = values - average
    spread = lax.optimization_barrier(jnp.mean(centred * centred, axis=-1, keepdims=True))
    return centred * lax.rsqrt(spread + EPSILON)

def two_layer(inputs, w_first, w_second):
    hidden_act = jnp.maximum(jnp.dot(inputs, w_first, preferred_element_type=jnp.float32), 0.0).astype(jnp.bfloat16)
    return jnp.dot(hidden_act, w_second, preferred_element_type=jnp.float32)

def coarse_layer(coarse_in, neighbour_list, w_edge_first, w_edge_second, w_node_first, w_node_second):
    row_count, latent_width = coarse_in.shape
    slot_valid = neighbour_list >= 0
    safe_index = jnp.where(slot_valid, neighbour_list, 0).astype(jnp.int32)
    sources = jnp.take(coarse_in, safe_index.reshape(-1), axis=0).reshape(row_count, -1, latent_width)
    sources = jnp.where(slot_valid[:, :, None], sources, jnp.zeros_like(sources))
    targets = jnp.broadcast_to(coarse_in[:, None, :], sources.shape)
    joined = jnp.concatenate([sources, targets], axis=-1).reshape(-1, 2 * latent_width)
    messages = layer_norm(two_layer(joined, w_edge_first, w_edge_second)).reshape(row_count, -1, latent_width)
    messages = jnp.where(slot_valid[:, :, None], messages, 0.0).astype(jnp.bfloat16)
    incoming = lax.optimization_barrier(jnp.sum(messages.astype(jnp.float32), axis=1)).astype(jnp.bfloat16)
    update = two_layer(jnp.concatenate([coarse_in, incoming], axis=-1), w_node_first, w_node_second)
    return (coarse_in.astype(jnp.float32) + layer_norm(update)).astype(jnp.bfloat16)

def reference(fine_nodes, fine_edges, fine_neighbours, group_send, halo_send, pool_send, pool_recv, coarse_neighbours, edge_in, edge_out, node_in, node_out, coarse_edge_in, coarse_edge_out, coarse_node_in, coarse_node_out):
    halo_four = halo_send.reshape(N_NODES, N_HIDDEN, N_NODES, SLOT)

    def one_device(device_index):
        group_index = (device_index // N_HIDDEN).astype(jnp.int32)
        share_index = (device_index % N_HIDDEN).astype(jnp.int32)
        first_row = (device_index * NS).astype(jnp.int32)
        own_rows = lax.dynamic_slice_in_dim(fine_nodes, first_row, NS, 0)
        own_edges = lax.dynamic_slice_in_dim(fine_edges, first_row, NS, 0)
        own_lists = lax.dynamic_slice_in_dim(fine_neighbours, first_row, NS, 0)
        group_lists = lax.dynamic_index_in_dim(group_send, group_index, 0, keepdims=False)
        wanted = lax.dynamic_index_in_dim(group_lists, share_index, 1, keepdims=False)
        group_rows = ((group_index * N_HIDDEN + jnp.arange(N_HIDDEN, dtype=jnp.int32))[:, None] * NS + wanted).reshape(-1).astype(jnp.int32)
        by_share = lax.dynamic_index_in_dim(halo_four, share_index, 1, keepdims=False)
        ghost_lists = lax.dynamic_index_in_dim(by_share, group_index, 1, keepdims=False)
        ghost_rows = ((jnp.arange(N_NODES, dtype=jnp.int32) * N_HIDDEN + share_index)[:, None] * NS + ghost_lists).reshape(-1).astype(jnp.int32)
        lookup_rows = jnp.concatenate([own_rows, jnp.take(fine_nodes, group_rows, axis=0), jnp.take(fine_nodes, ghost_rows, axis=0)], axis=0)
        slot_valid = own_lists >= 0
        safe_index = jnp.where(slot_valid, own_lists, 0).astype(jnp.int32)
        sources = jnp.take(lookup_rows, safe_index.reshape(-1), axis=0).reshape(NS, DEG, L)
        sources = jnp.where(slot_valid[:, :, None], sources, jnp.zeros_like(sources))
        targets = jnp.broadcast_to(own_rows[:, None, :], sources.shape)
        joined = jnp.concatenate([own_edges, sources, targets], axis=-1).reshape(-1, 3 * L)
        edge_sum = two_layer(joined, edge_in, edge_out).reshape(NS, DEG, L)
        new_edges = jnp.where(slot_valid[:, :, None], own_edges.astype(jnp.float32) + layer_norm(edge_sum), 0.0).astype(jnp.bfloat16)
        incoming = lax.optimization_barrier(jnp.sum(new_edges.astype(jnp.float32), axis=1)).astype(jnp.bfloat16)
        update = two_layer(jnp.concatenate([own_rows, incoming], axis=-1), node_in, node_out)
        fine_mid = (own_rows.astype(jnp.float32) + layer_norm(update)).astype(jnp.bfloat16)
        return (fine_mid, new_edges)
    fine_mid, edge_result = lax.map(one_device, jnp.arange(N_NODES * N_HIDDEN, dtype=jnp.int32))
    fine_mid = fine_mid.reshape(NF, L)
    edge_result = edge_result.reshape(NF, DEG, L)
    send_four = pool_send.reshape(N_NODES, N_HIDDEN, N_NODES, CAP)
    recv_four = jnp.transpose(pool_recv.reshape(N_NODES, N_HIDDEN, N_NODES, CAP), (2, 1, 0, 3))
    group_ids = jnp.arange(N_NODES, dtype=jnp.int32)[:, None, None, None]
    hidden_ids = jnp.arange(N_HIDDEN, dtype=jnp.int32)[None, :, None, None]
    owner_ids = jnp.arange(N_NODES, dtype=jnp.int32)[None, None, :, None]
    live_slot = send_four >= 0
    fine_index = jnp.where(live_slot, (group_ids * N_HIDDEN + hidden_ids) * NS + send_four, NF).astype(jnp.int32)
    coarse_index = jnp.where(live_slot, (owner_ids * N_HIDDEN + hidden_ids) * NC_DEV + recv_four, 0).astype(jnp.int32)
    cluster = jnp.zeros((NF + 1,), jnp.int32).at[fine_index.reshape(-1)].set(coarse_index.reshape(-1))[:NF]
    totals = jax.ops.segment_sum(fine_mid.astype(jnp.float32), cluster, num_segments=NC)
    counts = jax.ops.segment_sum(jnp.ones((NF,), jnp.float32), cluster, num_segments=NC)
    pooled = (totals / jnp.maximum(counts, 1.0)[:, None]).astype(jnp.bfloat16)

    def coarse_block(block_index):
        block_start = (block_index * N_HIDDEN * NC_DEV).astype(jnp.int32)
        block_rows = lax.dynamic_slice_in_dim(pooled, block_start, N_HIDDEN * NC_DEV, 0)
        block_lists = lax.dynamic_slice_in_dim(coarse_neighbours, block_start, N_HIDDEN * NC_DEV, 0)
        return jax.vmap(lambda rows_in, lists_in: coarse_layer(rows_in, lists_in, coarse_edge_in, coarse_edge_out, coarse_node_in, coarse_node_out))(block_rows.reshape(N_HIDDEN, NC_DEV, L), block_lists.reshape(N_HIDDEN, NC_DEV, DEG_C))
    coarse_result = lax.map(coarse_block, jnp.arange(N_NODES, dtype=jnp.int32)).reshape(NC, L)
    unpooled = jnp.take(coarse_result, cluster, axis=0)
    fine_result = (fine_mid.astype(jnp.float32) + unpooled.astype(jnp.float32)).astype(jnp.bfloat16)
    return (fine_result, edge_result, coarse_result)
```

```python
import jax
import jax.numpy as jnp
from jax import lax
from jax.experimental import pallas as pl
from jax.experimental.pallas import tpu as pltpu
from jax.sharding import PartitionSpec as P

EPSILON = 1e-05
MESH = pl.DeviceIdType.MESH
BF16 = jnp.bfloat16
F32 = jnp.float32
NX, NZ = 4, 16
NODES, HIDDEN = NX * NZ, 16
ROWS, WIDTH, UNITS = 128, 256, 1024
SLOTS = 6
EDGES = ROWS * SLOTS
COARSE = 16
COARSE_EDGES = COARSE * SLOTS
MSG = NODES * 8


def dot(a, b):
    return jnp.dot(a, b, preferred_element_type=F32)


def dot_nt(a, b):
    return lax.dot_general(a, b, (((1,), (1,)), ((), ())), preferred_element_type=F32)


def layer_norm(values):
    average = jnp.mean(values, axis=-1, keepdims=True)
    centred = values - average
    spread = jnp.mean(centred * centred, axis=-1, keepdims=True)
    return centred * lax.rsqrt(spread + EPSILON)


def iota(shape, dim):
    return lax.broadcasted_iota(jnp.int32, shape, dim)


def one_hot(condition):
    return jnp.where(condition, 1.0, 0.0).astype(BF16)


def spread_column(lists, rows, shift):
    slots, peers = lists.shape
    pick_peer = one_hot((iota((rows, peers), 0) >> shift) == iota((rows, peers), 1))
    table = dot_nt(pick_peer, lists.astype(F32).astype(BF16))
    slot = (iota((rows, slots), 0) & ((1 << shift) - 1)) >> 1
    return jnp.sum(
        jnp.where(slot == iota((rows, slots), 1), table, 0.0), axis=1, keepdims=True
    ).astype(jnp.int32)


def spread_row(lists, rows, shift):
    slots, peers = lists.shape
    pick_peer = one_hot((iota((peers, rows), 1) >> shift) == iota((peers, rows), 0))
    table = dot(lists.astype(F32).astype(BF16), pick_peer)
    slot = (iota((slots, rows), 1) & ((1 << shift) - 1)) >> 1
    return jnp.sum(
        jnp.where(slot == iota((slots, rows), 0), table, 0.0), axis=0, keepdims=True
    ).astype(jnp.int32)


def halves(rows):
    return jnp.concatenate([rows[:, :128], rows[:, 128:]], axis=0)


def row_picker(column):
    shape = (column.shape[0], 2 * ROWS)
    lane = iota(shape, 1)
    return one_hot((column == (lane & 127)) & ((iota(shape, 0) & 1) == (lane >> 7)))


def kernel(
    nodes_hbm, edges_hbm, neigh_hbm, group_hbm, halo_hbm, psend_hbm, precv_hbm, cneigh_hbm,
    w_ei_hbm, w_eo_hbm, w_ni_hbm, w_no_hbm, w_cei_hbm, w_ceo_hbm, w_cni_hbm, w_cno_hbm,
    fine_out, edge_out, coarse_out,
    nodes, edges, neigh, group, halo, psend, precv, cneigh,
    w_ei, w_eo, w_ni, w_no, w_cei, w_ceo, w_cni, w_cno,
    first_part, new_edges,
    group_src, group_dst, ghost_src, ghost_dst, pool_src, pool_dst, back_src, back_dst,
    load_sems, store_sem, send_sems, recv_sems,
):
    node_at = lax.axis_index("nodes")
    hidden_at = lax.axis_index("hidden")
    x_at = lax.div(node_at, NZ)
    z_at = lax.rem(node_at, NZ)

    barrier = pltpu.get_barrier_semaphore()

    def far_first(visit):
        def step(t, carry):
            away = (t + 1) >> 1
            dz = NZ // 2 + away * (1 - 2 * (t & 1))
            for dx in (2, 1, 3, 0):
                visit(lax.rem(x_at + dx, NX) * NZ + lax.rem(z_at + dz, NZ))
            return carry

        lax.fori_loop(0, NZ - 1, step, 0)
        for dx in (2, 1, 3):
            visit(lax.rem(x_at + dx, NX) * NZ + z_at)

    def group_first(visit):
        def step(t, carry):
            visit(lax.rem(hidden_at + t, HIDDEN))
            return carry

        lax.fori_loop(1, HIDDEN, step, 0)

    far_first(
        lambda p: pl.semaphore_signal(barrier, inc=1, device_id={"nodes": p}, device_id_type=MESH)
    )
    group_first(
        lambda p: pl.semaphore_signal(barrier, inc=1, device_id={"hidden": p}, device_id_type=MESH)
    )

    loads = []
    sources = (
        nodes_hbm, group_hbm.at[0, hidden_at], halo_hbm, psend_hbm, precv_hbm, neigh_hbm, cneigh_hbm,
        w_ei_hbm, edges_hbm, w_eo_hbm, w_ni_hbm, w_no_hbm, w_cei_hbm, w_ceo_hbm, w_cni_hbm, w_cno_hbm,
    )
    targets = (
        nodes, group, halo, psend, precv, neigh, cneigh,
        w_ei, edges, w_eo, w_ni, w_no, w_cei, w_ceo, w_cni, w_cno,
    )
    for i, (source, target) in enumerate(zip(sources, targets)):
        copy = pltpu.make_async_copy(source, target, load_sems.at[i])
        copy.start()
        loads.append(copy)

    for i in range(3):
        loads[i].wait()
    own = nodes[...]
    own_halves = halves(own)
    group_pick = row_picker(spread_column(group[...], HIDDEN * 16, 4))
    group_src[...] = dot(group_pick, own_halves).astype(BF16).reshape(HIDDEN, 16, 128)
    ghost_pick = row_picker(spread_column(halo[0], MSG, 3))
    ghost_src[...] = dot(ghost_pick, own_halves).reshape(NODES, 8, 128).astype(BF16)

    pl.semaphore_wait(barrier, NODES - 1 + HIDDEN - 1)

    def send(src, dst, which):
        def visit(p):
            pltpu.make_async_remote_copy(
                src_ref=src.at[p],
                dst_ref=dst.at[node_at],
                send_sem=send_sems.at[which],
                recv_sem=recv_sems.at[which],
                device_id={"nodes": p},
                device_id_type=MESH,
            ).start()

        far_first(visit)

    def send_group(p):
        pltpu.make_async_remote_copy(
            src_ref=group_src.at[p],
            dst_ref=group_dst.at[hidden_at],
            send_sem=send_sems.at[0],
            recv_sem=recv_sems.at[0],
            device_id={"hidden": p},
            device_id_type=MESH,
        ).start()

    def wait_all(buffer, count, sem):
        pltpu.make_async_copy(buffer.at[pl.ds(0, count)], buffer.at[pl.ds(0, count)], sem).wait()

    send(ghost_src, ghost_dst, 1)
    group_first(send_group)

    for i in range(3, 7):
        loads[i].wait()
    lists = jnp.concatenate(
        [neigh[...].astype(F32), jnp.zeros((ROWS - SLOTS, ROWS), F32)], axis=0
    )
    neigh_columns = lists.T.astype(jnp.int32)
    column = jnp.concatenate([neigh_columns[:, k : k + 1] for k in range(SLOTS)], axis=0)
    lane = iota((EDGES, ROWS), 1)
    take_own = one_hot(column == lane)
    take_group = one_hot(column == lane + ROWS)
    take_ghost = one_hot(column == lane + 2 * ROWS)
    valid = column >= 0

    send_column = spread_column(psend[0], MSG, 3)
    send_row = spread_row(psend[0], MSG, 3)
    pool_pick = row_picker(send_column)
    shape = (2 * ROWS, MSG)
    sub = iota(shape, 0)
    back_pick = one_hot((send_row == (sub & 127)) & ((iota(shape, 1) & 1) == (sub >> 7)))
    recv_column = spread_column(precv[0], MSG, 3)
    recv_row = spread_row(precv[0], MSG, 3)
    shape = (2 * COARSE, MSG)
    sub = iota(shape, 0)
    member = one_hot((recv_row == (sub & 15)) & ((iota(shape, 1) & 1) == (sub >> 4)))
    shape = (MSG, 2 * COARSE)
    lane = iota(shape, 1)
    member_back = one_hot((recv_column == (lane & 15)) & ((iota(shape, 0) & 1) == (lane >> 4)))
    counts = jnp.sum(member[:COARSE].astype(F32), axis=1, keepdims=True)
    scale_down = jnp.maximum(counts, 1.0)

    lists = jnp.concatenate(
        [cneigh[...].astype(F32), jnp.zeros((8 - SLOTS, COARSE), F32)], axis=0
    )
    lists = jnp.concatenate([lists, jnp.zeros((8, 128 - COARSE), F32)], axis=1)
    lists = jnp.concatenate([lists, jnp.zeros((120, 128), F32)], axis=0)
    coarse_columns = lists.T[:COARSE].astype(jnp.int32)
    coarse_column = jnp.concatenate(
        [coarse_columns[:, k : k + 1] for k in range(SLOTS)], axis=0
    )
    take_coarse = one_hot(coarse_column == iota((COARSE_EDGES, COARSE), 1))
    coarse_valid = coarse_column >= 0

    def half_of(shape, half, shift, slot_bits):
        row = iota(shape, 0)
        lane = iota(shape, 1)
        wanted = ((row >> slot_bits) << shift) + ((row & ((1 << slot_bits) - 1)) << 1) + half
        return one_hot(lane == wanted)

    group_split = [half_of((ROWS, HIDDEN * 16), half, 4, 3) for half in range(2)]
    ghost_split = [half_of((ROWS, MSG), half, 3, 1) for half in range(2)]

    loads[7].wait()
    loads[8].wait()
    from_target = dot(own, w_ei[2 * WIDTH :, :])
    for k in range(SLOTS):
        rows = pl.ds(k * ROWS, ROWS)
        first_part[rows, :] = dot(edges[rows, :], w_ei[:WIDTH, :]) + from_target
    for i in range(9, 16):
        loads[i].wait()
    node_part = dot(own, w_ni[:WIDTH, :])
    from_own = dot(take_own, own)

    group_dst[pl.ds(hidden_at, 1)] = group_src[pl.ds(hidden_at, 1)]
    wait_all(group_dst, HIDDEN - 1, recv_sems.at[0])
    arrived = group_dst[...].reshape(HIDDEN * 16, 128)
    in_group = jnp.concatenate([dot(split, arrived) for split in group_split], axis=1).astype(BF16)
    from_near = from_own + dot(take_group, in_group)

    ghost_dst[pl.ds(node_at, 1)] = ghost_src[pl.ds(node_at, 1)]
    wait_all(ghost_dst, NODES - 1, recv_sems.at[1])

    def flat(buffer):
        return buffer[...].astype(F32).reshape(MSG, 128).astype(BF16)

    arrived = flat(ghost_dst)
    ghosts = jnp.concatenate([dot(split, arrived) for split in ghost_split], axis=1).astype(BF16)
    source = (from_near + dot(take_ghost, ghosts)).astype(BF16)
    total = None
    for c in range(0, UNITS, WIDTH):
        hidden = first_part[:, c : c + WIDTH] + dot(source, w_ei[WIDTH : 2 * WIDTH, c : c + WIDTH])
        part = dot(jnp.maximum(hidden, 0.0).astype(BF16), w_eo[c : c + WIDTH, :])
        total = part if total is None else total + part
    result = jnp.where(valid, edges[...].astype(F32) + layer_norm(total), 0.0).astype(BF16)
    new_edges[...] = result
    store = pltpu.make_async_copy(new_edges, edge_out, store_sem)
    store.start()
    incoming = None
    for k in range(SLOTS):
        part = result[k * ROWS : (k + 1) * ROWS].astype(F32)
        incoming = part if incoming is None else incoming + part
    incoming = incoming.astype(BF16)
    hidden = jnp.maximum(node_part + dot(incoming, w_ni[WIDTH:, :]), 0.0).astype(BF16)
    fine_mid = (own.astype(F32) + layer_norm(dot(hidden, w_no[...]))).astype(BF16)

    pool_src[...] = dot(pool_pick, halves(fine_mid)).reshape(NODES, 8, 128).astype(BF16)
    send(pool_src, pool_dst, 2)
    pool_dst[pl.ds(node_at, 1)] = pool_src[pl.ds(node_at, 1)]
    wait_all(pool_dst, NODES - 1, recv_sems.at[2])

    sums = dot(member, flat(pool_dst))
    pooled = jnp.concatenate([sums[:COARSE], sums[COARSE:]], axis=1) / scale_down
    pooled = pooled.astype(BF16)
    from_target = dot(pooled, w_cei[WIDTH:, :])
    source = dot(take_coarse, pooled).astype(BF16)
    hidden = dot(source, w_cei[:WIDTH, :]) + jnp.concatenate([from_target] * SLOTS, axis=0)
    hidden = jnp.maximum(hidden, 0.0).astype(BF16)
    messages = jnp.where(coarse_valid, layer_norm(dot(hidden, w_ceo[...])), 0.0).astype(BF16)
    incoming = None
    for k in range(SLOTS):
        part = messages[k * COARSE : (k + 1) * COARSE].astype(F32)
        incoming = part if incoming is None else incoming + part
    incoming = incoming.astype(BF16)
    hidden = dot(pooled, w_cni[:WIDTH, :]) + dot(incoming, w_cni[WIDTH:, :])
    hidden = jnp.maximum(hidden, 0.0).astype(BF16)
    coarse = (pooled.astype(F32) + layer_norm(dot(hidden, w_cno[...]))).astype(BF16)
    coarse_out[...] = coarse

    back_src[...] = dot(member_back, halves(coarse)).reshape(NODES, 8, 128).astype(BF16)
    send(back_src, back_dst, 3)
    back_dst[pl.ds(node_at, 1)] = back_src[pl.ds(node_at, 1)]
    wait_all(back_dst, NODES - 1, recv_sems.at[3])

    returned = dot(back_pick, flat(back_dst))
    unpooled = jnp.concatenate([returned[:ROWS], returned[ROWS:]], axis=1)
    fine_out[...] = (fine_mid.astype(F32) + unpooled).astype(BF16)

    store.wait()
    wait_all(group_dst, HIDDEN - 1, send_sems.at[0])
    for which, buffer in ((1, ghost_dst), (2, pool_dst), (3, back_dst)):
        wait_all(buffer, NODES - 1, send_sems.at[which])


def shards(
    fine_nodes, fine_edges, fine_neighbours, group_send, halo_send, pool_send, pool_recv,
    coarse_neighbours, *weights,
):
    anywhere = pl.BlockSpec(memory_space=pl.ANY)
    in_vmem = pl.BlockSpec(memory_space=pltpu.VMEM)
    operands = (
        fine_nodes,
        fine_edges.transpose(1, 0, 2).reshape(EDGES, WIDTH),
        fine_neighbours.T,
        group_send.transpose(0, 1, 3, 2),
        halo_send.transpose(0, 2, 1),
        pool_send.transpose(0, 2, 1),
        pool_recv.transpose(0, 2, 1),
        coarse_neighbours.T,
    ) + weights
    message = pltpu.VMEM((NODES, 8, 128), BF16)
    group_message = pltpu.VMEM((HIDDEN, 16, 128), BF16)
    fine_result, edge_result, coarse_result = pl.pallas_call(
        kernel,
        out_shape=(
            jax.ShapeDtypeStruct((ROWS, WIDTH), BF16),
            jax.ShapeDtypeStruct((EDGES, WIDTH), BF16),
            jax.ShapeDtypeStruct((COARSE, WIDTH), BF16),
        ),
        in_specs=[anywhere] * len(operands),
        out_specs=(in_vmem, anywhere, in_vmem),
        scratch_shapes=[
            pltpu.VMEM((ROWS, WIDTH), BF16),
            pltpu.VMEM((EDGES, WIDTH), BF16),
            pltpu.VMEM((SLOTS, ROWS), jnp.int32),
            pltpu.VMEM((8, HIDDEN), jnp.int32),
            pltpu.VMEM((1, 2, NODES), jnp.int32),
            pltpu.VMEM((1, 4, NODES), jnp.int32),
            pltpu.VMEM((1, 4, NODES), jnp.int32),
            pltpu.VMEM((SLOTS, COARSE), jnp.int32),
        ]
        + [pltpu.VMEM(w.shape, BF16) for w in weights]
        + [
            pltpu.VMEM((EDGES, UNITS), F32),
            pltpu.VMEM((EDGES, WIDTH), BF16),
            group_message, group_message,
            message, message, message, message, message, message,
            pltpu.SemaphoreType.DMA((16,)),
            pltpu.SemaphoreType.DMA,
            pltpu.SemaphoreType.DMA((4,)),
            pltpu.SemaphoreType.DMA((4,)),
        ],
        compiler_params=pltpu.CompilerParams(
            collective_id=0, has_side_effects=True, vmem_limit_bytes=56 * 1024 * 1024
        ),
        cost_estimate=pl.CostEstimate(
            flops=2_100_000_000, bytes_accessed=8_000_000, transcendentals=2000
        ),
    )(*operands)
    edge_result = edge_result.reshape(SLOTS, ROWS, WIDTH).transpose(1, 0, 2)
    return fine_result, edge_result, coarse_result


def solution(mesh):
    rows = ("nodes", "hidden")
    in_specs = (
        P(rows, None),
        P(rows, None, None),
        P(rows, None),
        P("nodes", None, None, None),
        P(rows, None, None),
        P(rows, None, None),
        P(rows, None, None),
        P(rows, None),
    ) + (P(),) * 8
    out_specs = (P(rows, None), P(rows, None, None), P(rows, None))
    return jax.shard_map(shards, mesh=mesh, in_specs=in_specs, out_specs=out_specs, check_vma=False)
```

```python
import jax
import jax.numpy as jnp
from jax import lax
from jax.experimental import pallas as pl
from jax.experimental.pallas import tpu as pltpu
from jax.sharding import PartitionSpec as P

EPSILON = 1e-05
MESH = pl.DeviceIdType.MESH
BF16 = jnp.bfloat16
F32 = jnp.float32
NX, NZ = 4, 16
NODES, HIDDEN = NX * NZ, 16
ROWS, WIDTH, UNITS = 128, 256, 1024
SLOTS = 6
EDGES = ROWS * SLOTS
COARSE = 16
COARSE_EDGES = COARSE * SLOTS
MSG = NODES * 8


def dot(a, b):
    return jnp.dot(a, b, preferred_element_type=F32)


def dot_nt(a, b):
    return lax.dot_general(a, b, (((1,), (1,)), ((), ())), preferred_element_type=F32)


def layer_norm(values):
    average = jnp.mean(values, axis=-1, keepdims=True)
    centred = values - average
    spread = jnp.mean(centred * centred, axis=-1, keepdims=True)
    return centred * lax.rsqrt(spread + EPSILON)


def iota(shape, dim):
    return lax.broadcasted_iota(jnp.int32, shape, dim)


def one_hot(condition):
    return jnp.where(condition, 1.0, 0.0).astype(BF16)


def spread_column(lists, rows, shift):
    slots, peers = lists.shape
    pick_peer = one_hot((iota((rows, peers), 0) >> shift) == iota((rows, peers), 1))
    table = dot_nt(pick_peer, lists.astype(F32).astype(BF16))
    slot = (iota((rows, slots), 0) & ((1 << shift) - 1)) >> 1
    return jnp.sum(
        jnp.where(slot == iota((rows, slots), 1), table, 0.0), axis=1, keepdims=True
    ).astype(jnp.int32)


def spread_row(lists, rows, shift):
    slots, peers = lists.shape
    pick_peer = one_hot((iota((peers, rows), 1) >> shift) == iota((peers, rows), 0))
    table = dot(lists.astype(F32).astype(BF16), pick_peer)
    slot = (iota((slots, rows), 1) & ((1 << shift) - 1)) >> 1
    return jnp.sum(
        jnp.where(slot == iota((slots, rows), 0), table, 0.0), axis=0, keepdims=True
    ).astype(jnp.int32)


def halves(rows):
    return jnp.concatenate([rows[:, :128], rows[:, 128:]], axis=0)


def row_picker(column):
    shape = (column.shape[0], 2 * ROWS)
    lane = iota(shape, 1)
    return one_hot((column == (lane & 127)) & ((iota(shape, 0) & 1) == (lane >> 7)))


def kernel(
    nodes_hbm, edges_hbm, neigh_hbm, group_hbm, halo_hbm, psend_hbm, precv_hbm, cneigh_hbm,
    w_ei_hbm, w_eo_hbm, w_ni_hbm, w_no_hbm, w_cei_hbm, w_ceo_hbm, w_cni_hbm, w_cno_hbm,
    fine_out, edge_out, coarse_out,
    nodes, edges, neigh, group, halo, psend, precv, cneigh,
    w_ei, w_eo, w_ni, w_no, w_cei, w_ceo, w_cni, w_cno,
    first_part,
    group_src, group_dst, ghost_src, ghost_dst, pool_src, pool_dst, back_src, back_dst,
    load_sems, send_sems, recv_sems,
):
    node_at = lax.axis_index("nodes")
    hidden_at = lax.axis_index("hidden")
    x_at = lax.div(node_at, NZ)
    z_at = lax.rem(node_at, NZ)

    barrier = pltpu.get_barrier_semaphore()

    def far_first(visit):
        def step(t, carry):
            away = (t + 1) >> 1
            dz = NZ // 2 + away * (1 - 2 * (t & 1))
            for dx in (2, 1, 3, 0):
                visit(lax.rem(x_at + dx, NX) * NZ + lax.rem(z_at + dz, NZ))
            return carry

        lax.fori_loop(0, NZ - 1, step, 0)
        for dx in (2, 1, 3):
            visit(lax.rem(x_at + dx, NX) * NZ + z_at)

    def group_first(visit):
        def step(t, carry):
            visit(lax.rem(hidden_at + t, HIDDEN))
            return carry

        lax.fori_loop(1, HIDDEN, step, 0)

    far_first(
        lambda p: pl.semaphore_signal(barrier, inc=1, device_id={"nodes": p}, device_id_type=MESH)
    )
    group_first(
        lambda p: pl.semaphore_signal(barrier, inc=1, device_id={"hidden": p}, device_id_type=MESH)
    )

    loads = []
    sources = (
        nodes_hbm, group_hbm.at[0, hidden_at], halo_hbm, psend_hbm, precv_hbm, neigh_hbm, cneigh_hbm,
        w_ei_hbm, edges_hbm, w_eo_hbm, w_ni_hbm, w_no_hbm, w_cei_hbm, w_ceo_hbm, w_cni_hbm, w_cno_hbm,
    )
    targets = (
        nodes, group, halo, psend, precv, neigh, cneigh,
        w_ei, edges, w_eo, w_ni, w_no, w_cei, w_ceo, w_cni, w_cno,
    )
    for i, (source, target) in enumerate(zip(sources, targets)):
        copy = pltpu.make_async_copy(source, target, load_sems.at[i])
        copy.start()
        loads.append(copy)

    for i in range(3):
        loads[i].wait()
    own = nodes[...]
    own_halves = halves(own)
    group_pick = row_picker(spread_column(group[...], HIDDEN * 16, 4))
    group_src[...] = dot(group_pick, own_halves).astype(BF16).reshape(HIDDEN, 16, 128)
    ghost_pick = row_picker(spread_column(halo[0], MSG, 3))
    ghost_src[...] = dot(ghost_pick, own_halves).reshape(NODES, 8, 128)[:, :4].astype(BF16)

    pl.semaphore_wait(barrier, NODES - 1 + HIDDEN - 1)

    def send(src, dst, which):
        def visit(p):
            pltpu.make_async_remote_copy(
                src_ref=src.at[p],
                dst_ref=dst.at[node_at],
                send_sem=send_sems.at[which],
                recv_sem=recv_sems.at[which],
                device_id={"nodes": p},
                device_id_type=MESH,
            ).start()

        far_first(visit)

    def send_group(p):
        pltpu.make_async_remote_copy(
            src_ref=group_src.at[p],
            dst_ref=group_dst.at[hidden_at],
            send_sem=send_sems.at[0],
            recv_sem=recv_sems.at[0],
            device_id={"hidden": p},
            device_id_type=MESH,
        ).start()

    def wait_all(buffer, count, sem):
        pltpu.make_async_copy(buffer.at[pl.ds(0, count)], buffer.at[pl.ds(0, count)], sem).wait()

    send(ghost_src, ghost_dst, 1)
    group_first(send_group)

    for i in range(3, 7):
        loads[i].wait()
    lists = jnp.concatenate(
        [neigh[...].astype(F32), jnp.zeros((ROWS - SLOTS, ROWS), F32)], axis=0
    )
    neigh_columns = lists.T.astype(jnp.int32)
    column = jnp.concatenate([neigh_columns[:, k : k + 1] for k in range(SLOTS)], axis=0)
    lane = iota((EDGES, ROWS), 1)
    take_own = one_hot(column == lane)
    take_group = one_hot(column == lane + ROWS)
    take_ghost = one_hot(column == lane + 2 * ROWS)
    valid = column >= 0

    send_column = spread_column(psend[0], MSG, 3)
    send_row = spread_row(psend[0], MSG, 3)
    pool_pick = row_picker(send_column)
    shape = (2 * ROWS, MSG)
    sub = iota(shape, 0)
    back_pick = one_hot((send_row == (sub & 127)) & ((iota(shape, 1) & 1) == (sub >> 7)))
    recv_column = spread_column(precv[0], MSG, 3)
    recv_row = spread_row(precv[0], MSG, 3)
    shape = (2 * COARSE, MSG)
    sub = iota(shape, 0)
    member = one_hot((recv_row == (sub & 15)) & ((iota(shape, 1) & 1) == (sub >> 4)))
    shape = (MSG, 2 * COARSE)
    lane = iota(shape, 1)
    member_back = one_hot((recv_column == (lane & 15)) & ((iota(shape, 0) & 1) == (lane >> 4)))
    counts = jnp.sum(member[:COARSE].astype(F32), axis=1, keepdims=True)
    scale_down = jnp.maximum(counts, 1.0)

    lists = jnp.concatenate(
        [cneigh[...].astype(F32), jnp.zeros((8 - SLOTS, COARSE), F32)], axis=0
    )
    lists = jnp.concatenate([lists, jnp.zeros((8, 128 - COARSE), F32)], axis=1)
    lists = jnp.concatenate([lists, jnp.zeros((120, 128), F32)], axis=0)
    coarse_columns = lists.T[:COARSE].astype(jnp.int32)
    coarse_column = jnp.concatenate(
        [coarse_columns[:, k : k + 1] for k in range(SLOTS)], axis=0
    )
    take_coarse = one_hot(coarse_column == iota((COARSE_EDGES, COARSE), 1))
    coarse_valid = coarse_column >= 0

    def half_of(shape, half, shift, slot_bits):
        row = iota(shape, 0)
        lane = iota(shape, 1)
        wanted = ((row >> slot_bits) << shift) + ((row & ((1 << slot_bits) - 1)) << 1) + half
        return one_hot(lane == wanted)

    group_split = [half_of((ROWS, HIDDEN * 16), half, 4, 3) for half in range(2)]
    ghost_split = [half_of((ROWS, MSG), half, 3, 1) for half in range(2)]

    loads[7].wait()
    loads[8].wait()
    from_target = dot(own, w_ei[2 * WIDTH :, :])
    for k in range(SLOTS):
        rows = pl.ds(k * ROWS, ROWS)
        first_part[rows, :] = dot(edges[rows, :], w_ei[:WIDTH, :]) + from_target
    for i in range(9, 16):
        loads[i].wait()
    node_part = dot(own, w_ni[:WIDTH, :])
    from_own = dot(take_own, own)

    group_dst[pl.ds(hidden_at, 1)] = group_src[pl.ds(hidden_at, 1)]
    wait_all(group_dst, HIDDEN - 1, recv_sems.at[0])
    arrived = group_dst[...].reshape(HIDDEN * 16, 128)
    in_group = jnp.concatenate([dot(split, arrived) for split in group_split], axis=1).astype(BF16)
    from_near = from_own + dot(take_group, in_group)

    ghost_dst[pl.ds(node_at, 1)] = ghost_src[pl.ds(node_at, 1)]
    wait_all(ghost_dst, NODES - 1, recv_sems.at[1])

    def flat(buffer):
        return buffer[...].astype(F32).reshape(MSG, 128).astype(BF16)

    arrived = ghost_dst[...].astype(F32)
    arrived = jnp.concatenate([arrived, jnp.zeros_like(arrived)], axis=1)
    arrived = arrived.reshape(MSG, 128).astype(BF16)
    ghosts = jnp.concatenate([dot(split, arrived) for split in ghost_split], axis=1).astype(BF16)
    source = (from_near + dot(take_ghost, ghosts)).astype(BF16)
    total = None
    for c in range(0, UNITS, WIDTH):
        hidden = first_part[:, c : c + WIDTH] + dot(source, w_ei[WIDTH : 2 * WIDTH, c : c + WIDTH])
        part = dot(jnp.maximum(hidden, 0.0).astype(BF16), w_eo[c : c + WIDTH, :])
        total = part if total is None else total + part
    result = jnp.where(valid, edges[...].astype(F32) + layer_norm(total), 0.0).astype(BF16)
    edge_out[...] = result
    incoming = None
    for k in range(SLOTS):
        part = result[k * ROWS : (k + 1) * ROWS].astype(F32)
        incoming = part if incoming is None else incoming + part
    incoming = incoming.astype(BF16)
    hidden = jnp.maximum(node_part + dot(incoming, w_ni[WIDTH:, :]), 0.0).astype(BF16)
    fine_mid = (own.astype(F32) + layer_norm(dot(hidden, w_no[...]))).astype(BF16)

    pool_src[...] = dot(pool_pick, halves(fine_mid)).reshape(NODES, 8, 128).astype(BF16)
    send(pool_src, pool_dst, 2)
    pool_dst[pl.ds(node_at, 1)] = pool_src[pl.ds(node_at, 1)]
    wait_all(pool_dst, NODES - 1, recv_sems.at[2])

    sums = dot(member, flat(pool_dst))
    pooled = jnp.concatenate([sums[:COARSE], sums[COARSE:]], axis=1) / scale_down
    pooled = pooled.astype(BF16)
    from_target = dot(pooled, w_cei[WIDTH:, :])
    source = dot(take_coarse, pooled).astype(BF16)
    hidden = dot(source, w_cei[:WIDTH, :]) + jnp.concatenate([from_target] * SLOTS, axis=0)
    hidden = jnp.maximum(hidden, 0.0).astype(BF16)
    messages = jnp.where(coarse_valid, layer_norm(dot(hidden, w_ceo[...])), 0.0).astype(BF16)
    incoming = None
    for k in range(SLOTS):
        part = messages[k * COARSE : (k + 1) * COARSE].astype(F32)
        incoming = part if incoming is None else incoming + part
    incoming = incoming.astype(BF16)
    hidden = dot(pooled, w_cni[:WIDTH, :]) + dot(incoming, w_cni[WIDTH:, :])
    hidden = jnp.maximum(hidden, 0.0).astype(BF16)
    coarse = (pooled.astype(F32) + layer_norm(dot(hidden, w_cno[...]))).astype(BF16)
    coarse_out[...] = coarse

    back_src[...] = dot(member_back, halves(coarse)).reshape(NODES, 8, 128).astype(BF16)
    send(back_src, back_dst, 3)
    back_dst[pl.ds(node_at, 1)] = back_src[pl.ds(node_at, 1)]
    wait_all(back_dst, NODES - 1, recv_sems.at[3])

    returned = dot(back_pick, flat(back_dst))
    unpooled = jnp.concatenate([returned[:ROWS], returned[ROWS:]], axis=1)
    fine_out[...] = (fine_mid.astype(F32) + unpooled).astype(BF16)

    wait_all(group_dst, HIDDEN - 1, send_sems.at[0])
    for which, buffer in ((1, ghost_dst), (2, pool_dst), (3, back_dst)):
        wait_all(buffer, NODES - 1, send_sems.at[which])


def hand_over(*refs):
    sems = refs[-1]
    copies = [pltpu.make_async_copy(refs[i], refs[3 + i], sems.at[i]) for i in range(3)]
    for copy in copies:
        copy.start()
    for copy in copies:
        copy.wait()


def shards(
    fine_nodes, fine_edges, fine_neighbours, group_send, halo_send, pool_send, pool_recv,
    coarse_neighbours, *weights,
):
    anywhere = pl.BlockSpec(memory_space=pl.ANY)
    in_vmem = pl.BlockSpec(memory_space=pltpu.VMEM)
    operands = (
        fine_nodes,
        fine_edges.transpose(1, 0, 2).reshape(EDGES, WIDTH),
        fine_neighbours.T,
        group_send.transpose(0, 1, 3, 2),
        halo_send.transpose(0, 2, 1),
        pool_send.transpose(0, 2, 1),
        pool_recv.transpose(0, 2, 1),
        coarse_neighbours.T,
    ) + weights
    message = pltpu.VMEM((NODES, 8, 128), BF16)
    group_message = pltpu.VMEM((HIDDEN, 16, 128), BF16)
    results = (
        jax.ShapeDtypeStruct((ROWS, WIDTH), BF16),
        jax.ShapeDtypeStruct((EDGES, WIDTH), BF16),
        jax.ShapeDtypeStruct((COARSE, WIDTH), BF16),
    )
    held = pl.pallas_call(
        kernel,
        out_shape=tuple(pltpu.VMEM(r.shape, BF16) for r in results),
        in_specs=[anywhere] * len(operands),
        out_specs=(in_vmem,) * 3,
        scratch_shapes=[
            pltpu.VMEM((ROWS, WIDTH), BF16),
            pltpu.VMEM((EDGES, WIDTH), BF16),
            pltpu.VMEM((SLOTS, ROWS), jnp.int32),
            pltpu.VMEM((8, HIDDEN), jnp.int32),
            pltpu.VMEM((1, 2, NODES), jnp.int32),
            pltpu.VMEM((1, 4, NODES), jnp.int32),
            pltpu.VMEM((1, 4, NODES), jnp.int32),
            pltpu.VMEM((SLOTS, COARSE), jnp.int32),
        ]
        + [pltpu.VMEM(w.shape, BF16) for w in weights]
        + [
            pltpu.VMEM((EDGES, UNITS), F32),
            group_message, group_message,
            pltpu.VMEM((NODES, 4, 128), BF16), pltpu.VMEM((NODES, 4, 128), BF16),
            message, message, message, message,
            pltpu.SemaphoreType.DMA((16,)),
            pltpu.SemaphoreType.DMA((4,)),
            pltpu.SemaphoreType.DMA((4,)),
        ],
        compiler_params=pltpu.CompilerParams(
            collective_id=0, has_side_effects=True, vmem_limit_bytes=56 * 1024 * 1024
        ),
        cost_estimate=pl.CostEstimate(
            flops=2_100_000_000, bytes_accessed=8_000_000, transcendentals=2000
        ),
    )(*operands)
    fine_result, edge_result, coarse_result = pl.pallas_call(
        hand_over,
        out_shape=results,
        in_specs=[in_vmem] * 3,
        out_specs=(pl.BlockSpec(memory_space=pltpu.HBM),) * 3,
        scratch_shapes=[pltpu.SemaphoreType.DMA((3,))],
        compiler_params=pltpu.CompilerParams(vmem_limit_bytes=56 * 1024 * 1024),
    )(*[pltpu.with_memory_space_constraint(h, pltpu.VMEM) for h in held])
    edge_result = edge_result.reshape(SLOTS, ROWS, WIDTH).transpose(1, 0, 2)
    return fine_result, edge_result, coarse_result


def solution(mesh):
    rows = ("nodes", "hidden")
    in_specs = (
        P(rows, None),
        P(rows, None, None),
        P(rows, None),
        P("nodes", None, None, None),
        P(rows, None, None),
        P(rows, None, None),
        P(rows, None, None),
        P(rows, None),
    ) + (P(),) * 8
    out_specs = (P(rows, None), P(rows, None, None), P(rows, None))
    return jax.shard_map(shards, mesh=mesh, in_specs=in_specs, out_specs=out_specs, check_vma=False)
```

```python
import jax
import jax.numpy as jnp
from jax import lax
from jax.experimental import pallas as pl
from jax.experimental.pallas import tpu as pltpu
from jax.sharding import PartitionSpec as P

EPSILON = 1e-05
MESH = pl.DeviceIdType.MESH
BF16 = jnp.bfloat16
F32 = jnp.float32
NX, NZ = 4, 16
NODES, HIDDEN = NX * NZ, 16
ROWS, WIDTH, UNITS = 128, 256, 1024
SLOTS = 6
EDGES = ROWS * SLOTS
COARSE = 16
COARSE_EDGES = COARSE * SLOTS
MSG = NODES * 8


def dot(a, b):
    return jnp.dot(a, b, preferred_element_type=F32)


def dot_nt(a, b):
    return lax.dot_general(a, b, (((1,), (1,)), ((), ())), preferred_element_type=F32)


def layer_norm(values):
    average = jnp.mean(values, axis=-1, keepdims=True)
    centred = values - average
    spread = jnp.mean(centred * centred, axis=-1, keepdims=True)
    return centred * lax.rsqrt(spread + EPSILON)


def iota(shape, dim):
    return lax.broadcasted_iota(jnp.int32, shape, dim)


def one_hot(condition):
    return jnp.where(condition, 1.0, 0.0).astype(BF16)


def spread_column(lists, rows, shift):
    slots, peers = lists.shape
    pick_peer = one_hot((iota((rows, peers), 0) >> shift) == iota((rows, peers), 1))
    table = dot_nt(pick_peer, lists.astype(F32).astype(BF16))
    slot = (iota((rows, slots), 0) & ((1 << shift) - 1)) >> 1
    return jnp.sum(
        jnp.where(slot == iota((rows, slots), 1), table, 0.0), axis=1, keepdims=True
    ).astype(jnp.int32)


def spread_row(lists, rows, shift):
    slots, peers = lists.shape
    pick_peer = one_hot((iota((peers, rows), 1) >> shift) == iota((peers, rows), 0))
    table = dot(lists.astype(F32).astype(BF16), pick_peer)
    slot = (iota((slots, rows), 1) & ((1 << shift) - 1)) >> 1
    return jnp.sum(
        jnp.where(slot == iota((slots, rows), 0), table, 0.0), axis=0, keepdims=True
    ).astype(jnp.int32)


def halves(rows):
    return jnp.concatenate([rows[:, :128], rows[:, 128:]], axis=0)


def row_picker(column):
    shape = (column.shape[0], 2 * ROWS)
    lane = iota(shape, 1)
    return one_hot((column == (lane & 127)) & ((iota(shape, 0) & 1) == (lane >> 7)))


def kernel(
    nodes_hbm, edges_hbm, neigh_hbm, group_hbm, halo_hbm, psend_hbm, precv_hbm, cneigh_hbm,
    w_ei_hbm, w_eo_hbm, w_ni_hbm, w_no_hbm, w_cei_hbm, w_ceo_hbm, w_cni_hbm, w_cno_hbm,
    fine_out, edge_out, coarse_out,
    nodes, edges, neigh, group, halo, psend, precv, cneigh,
    w_ei, w_eo, w_ni, w_no, w_cei, w_ceo, w_cni, w_cno,
    first_part,
    group_src, group_dst, ghost_src, ghost_dst, pool_src, pool_dst, back_src, back_dst,
    load_sems, send_sems, recv_sems,
):
    node_at = lax.axis_index("nodes")
    hidden_at = lax.axis_index("hidden")
    x_at = lax.div(node_at, NZ)
    z_at = lax.rem(node_at, NZ)

    barrier = pltpu.get_barrier_semaphore()

    def far_first(visit):
        def step(t, carry):
            away = (t + 1) >> 1
            dz = NZ // 2 + away * (1 - 2 * (t & 1))
            for dx in (2, 1, 3, 0):
                visit(lax.rem(x_at + dx, NX) * NZ + lax.rem(z_at + dz, NZ))
            return carry

        lax.fori_loop(0, NZ - 1, step, 0)
        for dx in (2, 1, 3):
            visit(lax.rem(x_at + dx, NX) * NZ + z_at)

    def group_first(visit):
        def step(t, carry):
            away = (t + 1) >> 1
            visit(lax.rem(hidden_at + HIDDEN // 2 + away * (1 - 2 * (t & 1)), HIDDEN))
            return carry

        lax.fori_loop(0, HIDDEN - 1, step, 0)

    far_first(
        lambda p: pl.semaphore_signal(barrier, inc=1, device_id={"nodes": p}, device_id_type=MESH)
    )
    group_first(
        lambda p: pl.semaphore_signal(barrier, inc=1, device_id={"hidden": p}, device_id_type=MESH)
    )

    loads = []
    sources = (
        nodes_hbm, group_hbm.at[0, hidden_at], halo_hbm, psend_hbm, precv_hbm, neigh_hbm, cneigh_hbm,
        w_ei_hbm, edges_hbm, w_eo_hbm, w_ni_hbm, w_no_hbm, w_cei_hbm, w_ceo_hbm, w_cni_hbm, w_cno_hbm,
    )
    targets = (
        nodes, group, halo, psend, precv, neigh, cneigh,
        w_ei, edges, w_eo, w_ni, w_no, w_cei, w_ceo, w_cni, w_cno,
    )
    for i, (source, target) in enumerate(zip(sources, targets)):
        copy = pltpu.make_async_copy(source, target, load_sems.at[i])
        copy.start()
        loads.append(copy)

    for i in range(3):
        loads[i].wait()
    own = nodes[...]
    own_halves = halves(own)
    group_pick = row_picker(spread_column(group[...], HIDDEN * 16, 4))
    group_src[...] = dot(group_pick, own_halves).astype(BF16).reshape(HIDDEN, 16, 128)
    ghost_pick = row_picker(spread_column(halo[0], MSG, 3))
    ghost_src[...] = dot(ghost_pick, own_halves).reshape(NODES, 8, 128)[:, :4].astype(BF16)

    pl.semaphore_wait(barrier, NODES - 1 + HIDDEN - 1)

    def low_first(visit):
        def step(z, carry):
            for dx in (2, 1, 3):
                visit(lax.rem(x_at + dx, NX) * NZ + z)

            @pl.when(z != z_at)
            def _():
                visit(x_at * NZ + z)

            return carry

        lax.fori_loop(0, NZ, step, 0)

    def send(src, dst, which, order=far_first):
        def visit(p):
            pltpu.make_async_remote_copy(
                src_ref=src.at[p],
                dst_ref=dst.at[node_at],
                send_sem=send_sems.at[which],
                recv_sem=recv_sems.at[which],
                device_id={"nodes": p},
                device_id_type=MESH,
            ).start()

        order(visit)

    def send_group(p):
        pltpu.make_async_remote_copy(
            src_ref=group_src.at[p],
            dst_ref=group_dst.at[hidden_at],
            send_sem=send_sems.at[0],
            recv_sem=recv_sems.at[0],
            device_id={"hidden": p},
            device_id_type=MESH,
        ).start()

    def wait_all(buffer, count, sem):
        pltpu.make_async_copy(buffer.at[pl.ds(0, count)], buffer.at[pl.ds(0, count)], sem).wait()

    group_first(send_group)
    send(ghost_src, ghost_dst, 1)

    for i in range(3, 7):
        loads[i].wait()
    lists = jnp.concatenate(
        [neigh[...].astype(F32), jnp.zeros((ROWS - SLOTS, ROWS), F32)], axis=0
    )
    neigh_columns = lists.T.astype(jnp.int32)
    column = jnp.concatenate([neigh_columns[:, k : k + 1] for k in range(SLOTS)], axis=0)
    lane = iota((EDGES, ROWS), 1)
    take_own = one_hot(column == lane)
    take_group = one_hot(column == lane + ROWS)
    take_ghost = one_hot(column == lane + 2 * ROWS)
    valid = column >= 0

    send_column = spread_column(psend[0], MSG, 3)
    send_row = spread_row(psend[0], MSG, 3)
    pool_pick = row_picker(send_column)
    shape = (2 * ROWS, MSG)
    sub = iota(shape, 0)
    back_pick = one_hot((send_row == (sub & 127)) & ((iota(shape, 1) & 1) == (sub >> 7)))
    recv_column = spread_column(precv[0], MSG, 3)
    recv_row = spread_row(precv[0], MSG, 3)
    shape = (2 * COARSE, MSG)
    sub = iota(shape, 0)
    member = one_hot((recv_row == (sub & 15)) & ((iota(shape, 1) & 1) == (sub >> 4)))
    shape = (MSG, 2 * COARSE)
    lane = iota(shape, 1)
    member_back = one_hot((recv_column == (lane & 15)) & ((iota(shape, 0) & 1) == (lane >> 4)))
    counts = jnp.sum(member[:COARSE].astype(F32), axis=1, keepdims=True)
    scale_down = jnp.maximum(counts, 1.0)

    lists = jnp.concatenate(
        [cneigh[...].astype(F32), jnp.zeros((8 - SLOTS, COARSE), F32)], axis=0
    )
    lists = jnp.concatenate([lists, jnp.zeros((8, 128 - COARSE), F32)], axis=1)
    lists = jnp.concatenate([lists, jnp.zeros((120, 128), F32)], axis=0)
    coarse_columns = lists.T[:COARSE].astype(jnp.int32)
    coarse_column = jnp.concatenate(
        [coarse_columns[:, k : k + 1] for k in range(SLOTS)], axis=0
    )
    take_coarse = one_hot(coarse_column == iota((COARSE_EDGES, COARSE), 1))
    coarse_valid = coarse_column >= 0

    def half_of(shape, half, shift, slot_bits):
        row = iota(shape, 0)
        lane = iota(shape, 1)
        wanted = ((row >> slot_bits) << shift) + ((row & ((1 << slot_bits) - 1)) << 1) + half
        return one_hot(lane == wanted)

    group_split = [half_of((ROWS, HIDDEN * 16), half, 4, 3) for half in range(2)]
    ghost_split = [half_of((ROWS, MSG), half, 3, 1) for half in range(2)]

    loads[7].wait()
    loads[8].wait()
    from_target = dot(own, w_ei[2 * WIDTH :, :])
    for k in range(SLOTS):
        rows = pl.ds(k * ROWS, ROWS)
        first_part[rows, :] = dot(edges[rows, :], w_ei[:WIDTH, :]) + from_target
    for i in range(9, 16):
        loads[i].wait()
    node_part = dot(own, w_ni[:WIDTH, :])
    from_own = dot(take_own, own)

    group_dst[pl.ds(hidden_at, 1)] = group_src[pl.ds(hidden_at, 1)]
    wait_all(group_dst, HIDDEN - 1, recv_sems.at[0])
    arrived = group_dst[...].reshape(HIDDEN * 16, 128)
    in_group = jnp.concatenate([dot(split, arrived) for split in group_split], axis=1).astype(BF16)
    from_near = from_own + dot(take_group, in_group)

    ghost_dst[pl.ds(node_at, 1)] = ghost_src[pl.ds(node_at, 1)]
    wait_all(ghost_dst, NODES - 1, recv_sems.at[1])

    def flat(buffer):
        return buffer[...].astype(F32).reshape(MSG, 128).astype(BF16)

    arrived = ghost_dst[...].astype(F32)
    arrived = jnp.concatenate([arrived, jnp.zeros_like(arrived)], axis=1)
    arrived = arrived.reshape(MSG, 128).astype(BF16)
    ghosts = jnp.concatenate([dot(split, arrived) for split in ghost_split], axis=1).astype(BF16)
    source = (from_near + dot(take_ghost, ghosts)).astype(BF16)
    total = None
    for c in range(0, UNITS, WIDTH):
        hidden = first_part[:, c : c + WIDTH] + dot(source, w_ei[WIDTH : 2 * WIDTH, c : c + WIDTH])
        part = dot(jnp.maximum(hidden, 0.0).astype(BF16), w_eo[c : c + WIDTH, :])
        total = part if total is None else total + part
    result = jnp.where(valid, edges[...].astype(F32) + layer_norm(total), 0.0).astype(BF16)
    edge_out[...] = result
    incoming = None
    for k in range(SLOTS):
        part = result[k * ROWS : (k + 1) * ROWS].astype(F32)
        incoming = part if incoming is None else incoming + part
    incoming = incoming.astype(BF16)
    hidden = jnp.maximum(node_part + dot(incoming, w_ni[WIDTH:, :]), 0.0).astype(BF16)
    fine_mid = (own.astype(F32) + layer_norm(dot(hidden, w_no[...]))).astype(BF16)

    pool_src[...] = dot(pool_pick, halves(fine_mid)).reshape(NODES, 8, 128).astype(BF16)
    send(pool_src, pool_dst, 2)
    pool_dst[pl.ds(node_at, 1)] = pool_src[pl.ds(node_at, 1)]
    wait_all(pool_dst, NODES - 1, recv_sems.at[2])

    sums = dot(member, flat(pool_dst))
    pooled = jnp.concatenate([sums[:COARSE], sums[COARSE:]], axis=1) / scale_down
    pooled = pooled.astype(BF16)
    from_target = dot(pooled, w_cei[WIDTH:, :])
    source = dot(take_coarse, pooled).astype(BF16)
    hidden = dot(source, w_cei[:WIDTH, :]) + jnp.concatenate([from_target] * SLOTS, axis=0)
    hidden = jnp.maximum(hidden, 0.0).astype(BF16)
    messages = jnp.where(coarse_valid, layer_norm(dot(hidden, w_ceo[...])), 0.0).astype(BF16)
    incoming = None
    for k in range(SLOTS):
        part = messages[k * COARSE : (k + 1) * COARSE].astype(F32)
        incoming = part if incoming is None else incoming + part
    incoming = incoming.astype(BF16)
    hidden = dot(pooled, w_cni[:WIDTH, :]) + dot(incoming, w_cni[WIDTH:, :])
    hidden = jnp.maximum(hidden, 0.0).astype(BF16)
    coarse = (pooled.astype(F32) + layer_norm(dot(hidden, w_cno[...]))).astype(BF16)
    coarse_out[...] = coarse

    back_src[...] = dot(member_back, halves(coarse)).reshape(NODES, 8, 128).astype(BF16)
    send(back_src, back_dst, 3, low_first)
    back_dst[pl.ds(node_at, 1)] = back_src[pl.ds(node_at, 1)]
    wait_all(back_dst, NODES - 1, recv_sems.at[3])

    returned = dot(back_pick, flat(back_dst))
    unpooled = jnp.concatenate([returned[:ROWS], returned[ROWS:]], axis=1)
    fine_out[...] = (fine_mid.astype(F32) + unpooled).astype(BF16)

    wait_all(group_dst, HIDDEN - 1, send_sems.at[0])
    for which, buffer in ((1, ghost_dst), (2, pool_dst), (3, back_dst)):
        wait_all(buffer, NODES - 1, send_sems.at[which])


def hand_over(*refs):
    sems = refs[-1]
    copies = [pltpu.make_async_copy(refs[i], refs[3 + i], sems.at[i]) for i in range(3)]
    for copy in copies:
        copy.start()
    for copy in copies:
        copy.wait()


def shards(
    fine_nodes, fine_edges, fine_neighbours, group_send, halo_send, pool_send, pool_recv,
    coarse_neighbours, *weights,
):
    anywhere = pl.BlockSpec(memory_space=pl.ANY)
    in_vmem = pl.BlockSpec(memory_space=pltpu.VMEM)
    operands = (
        fine_nodes,
        fine_edges.transpose(1, 0, 2).reshape(EDGES, WIDTH),
        fine_neighbours.T,
        group_send.transpose(0, 1, 3, 2),
        halo_send.transpose(0, 2, 1),
        pool_send.transpose(0, 2, 1),
        pool_recv.transpose(0, 2, 1),
        coarse_neighbours.T,
    ) + weights
    message = pltpu.VMEM((NODES, 8, 128), BF16)
    group_message = pltpu.VMEM((HIDDEN, 16, 128), BF16)
    results = (
        jax.ShapeDtypeStruct((ROWS, WIDTH), BF16),
        jax.ShapeDtypeStruct((EDGES, WIDTH), BF16),
        jax.ShapeDtypeStruct((COARSE, WIDTH), BF16),
    )
    held = pl.pallas_call(
        kernel,
        out_shape=tuple(pltpu.VMEM(r.shape, BF16) for r in results),
        in_specs=[anywhere] * len(operands),
        out_specs=(in_vmem,) * 3,
        scratch_shapes=[
            pltpu.VMEM((ROWS, WIDTH), BF16),
            pltpu.VMEM((EDGES, WIDTH), BF16),
            pltpu.VMEM((SLOTS, ROWS), jnp.int32),
            pltpu.VMEM((8, HIDDEN), jnp.int32),
            pltpu.VMEM((1, 2, NODES), jnp.int32),
            pltpu.VMEM((1, 4, NODES), jnp.int32),
            pltpu.VMEM((1, 4, NODES), jnp.int32),
            pltpu.VMEM((SLOTS, COARSE), jnp.int32),
        ]
        + [pltpu.VMEM(w.shape, BF16) for w in weights]
        + [
            pltpu.VMEM((EDGES, UNITS), F32),
            group_message, group_message,
            pltpu.VMEM((NODES, 4, 128), BF16), pltpu.VMEM((NODES, 4, 128), BF16),
            message, message, message, message,
            pltpu.SemaphoreType.DMA((16,)),
            pltpu.SemaphoreType.DMA((4,)),
            pltpu.SemaphoreType.DMA((4,)),
        ],
        compiler_params=pltpu.CompilerParams(
            collective_id=0, has_side_effects=True, vmem_limit_bytes=56 * 1024 * 1024
        ),
        cost_estimate=pl.CostEstimate(
            flops=2_100_000_000, bytes_accessed=8_000_000, transcendentals=2000
        ),
    )(*operands)
    fine_result, edge_result, coarse_result = pl.pallas_call(
        hand_over,
        out_shape=results,
        in_specs=[in_vmem] * 3,
        out_specs=(pl.BlockSpec(memory_space=pltpu.HBM),) * 3,
        scratch_shapes=[pltpu.SemaphoreType.DMA((3,))],
        compiler_params=pltpu.CompilerParams(vmem_limit_bytes=56 * 1024 * 1024),
    )(*[pltpu.with_memory_space_constraint(h, pltpu.VMEM) for h in held])
    edge_result = edge_result.reshape(SLOTS, ROWS, WIDTH).transpose(1, 0, 2)
    return fine_result, edge_result, coarse_result


def solution(mesh):
    rows = ("nodes", "hidden")
    in_specs = (
        P(rows, None),
        P(rows, None, None),
        P(rows, None),
        P("nodes", None, None, None),
        P(rows, None, None),
        P(rows, None, None),
        P(rows, None, None),
        P(rows, None),
    ) + (P(),) * 8
    out_specs = (P(rows, None), P(rows, None, None), P(rows, None))
    return jax.shard_map(shards, mesh=mesh, in_specs=in_specs, out_specs=out_specs, check_vma=False)
```

```python
import jax
import jax.numpy as jnp
from jax import lax
from jax.experimental import pallas as pl
from jax.experimental.pallas import tpu as pltpu
from jax.sharding import PartitionSpec as P

EPSILON = 1e-05
MESH = pl.DeviceIdType.MESH
BF16 = jnp.bfloat16
F32 = jnp.float32
NX, NZ = 4, 16
NODES, HIDDEN = NX * NZ, 16
ROWS, WIDTH, UNITS = 128, 256, 1024
SLOTS = 6
EDGES = ROWS * SLOTS
COARSE = 16
COARSE_EDGES = COARSE * SLOTS
MSG = NODES * 8


def dot(a, b):
    return jnp.dot(a, b, preferred_element_type=F32)


def dot_nt(a, b):
    return lax.dot_general(a, b, (((1,), (1,)), ((), ())), preferred_element_type=F32)


def layer_norm(values):
    average = jnp.mean(values, axis=-1, keepdims=True)
    centred = values - average
    spread = jnp.mean(centred * centred, axis=-1, keepdims=True)
    return centred * lax.rsqrt(spread + EPSILON)


def iota(shape, dim):
    return lax.broadcasted_iota(jnp.int32, shape, dim)


def one_hot(condition):
    return jnp.where(condition, 1.0, 0.0).astype(BF16)


def spread_column(lists, rows, shift):
    slots, peers = lists.shape
    pick_peer = one_hot((iota((rows, peers), 0) >> shift) == iota((rows, peers), 1))
    table = dot_nt(pick_peer, lists.astype(F32).astype(BF16))
    slot = (iota((rows, slots), 0) & ((1 << shift) - 1)) >> 1
    return jnp.sum(
        jnp.where(slot == iota((rows, slots), 1), table, 0.0), axis=1, keepdims=True
    ).astype(jnp.int32)


def spread_row(lists, rows, shift):
    slots, peers = lists.shape
    pick_peer = one_hot((iota((peers, rows), 1) >> shift) == iota((peers, rows), 0))
    table = dot(lists.astype(F32).astype(BF16), pick_peer)
    slot = (iota((slots, rows), 1) & ((1 << shift) - 1)) >> 1
    return jnp.sum(
        jnp.where(slot == iota((slots, rows), 0), table, 0.0), axis=0, keepdims=True
    ).astype(jnp.int32)


def halves(rows):
    return jnp.concatenate([rows[:, :128], rows[:, 128:]], axis=0)


def row_picker(column):
    shape = (column.shape[0], 2 * ROWS)
    lane = iota(shape, 1)
    return one_hot((column == (lane & 127)) & ((iota(shape, 0) & 1) == (lane >> 7)))


def kernel(
    nodes_hbm, edges_hbm, neigh_hbm, group_hbm, halo_hbm, psend_hbm, precv_hbm, cneigh_hbm,
    w_ei_hbm, w_eo_hbm, w_ni_hbm, w_no_hbm, w_cei_hbm, w_ceo_hbm, w_cni_hbm, w_cno_hbm,
    fine_out, edge_out, coarse_out,
    nodes, edges, neigh, group, halo, psend, precv, cneigh,
    w_ei, w_eo, w_ni, w_no, w_cei, w_ceo, w_cni, w_cno,
    first_part,
    group_src, group_dst, ghost_src, ghost_dst, pool_src, pool_dst, back_src, back_dst,
    load_sems, send_sems, recv_sems,
):
    node_at = lax.axis_index("nodes")
    hidden_at = lax.axis_index("hidden")
    x_at = lax.div(node_at, NZ)
    z_at = lax.rem(node_at, NZ)

    barrier = pltpu.get_barrier_semaphore()

    def far_first(visit):
        def step(t, carry):
            away = (t + 1) >> 1
            dz = NZ // 2 + away * (1 - 2 * (t & 1))
            for dx in (2, 1, 3, 0):
                visit(lax.rem(x_at + dx, NX) * NZ + lax.rem(z_at + dz, NZ))
            return carry

        lax.fori_loop(0, NZ - 1, step, 0, unroll=5)
        for dx in (2, 1, 3):
            visit(lax.rem(x_at + dx, NX) * NZ + z_at)

    def group_first(visit):
        def step(t, carry):
            away = (t + 1) >> 1
            visit(lax.rem(hidden_at + HIDDEN // 2 + away * (1 - 2 * (t & 1)), HIDDEN))
            return carry

        lax.fori_loop(0, HIDDEN - 1, step, 0, unroll=5)

    far_first(
        lambda p: pl.semaphore_signal(barrier, inc=1, device_id={"nodes": p}, device_id_type=MESH)
    )
    group_first(
        lambda p: pl.semaphore_signal(barrier, inc=1, device_id={"hidden": p}, device_id_type=MESH)
    )

    loads = []
    sources = (
        nodes_hbm, group_hbm.at[0, hidden_at], halo_hbm, psend_hbm, precv_hbm, neigh_hbm, cneigh_hbm,
        w_ei_hbm, edges_hbm, w_eo_hbm, w_ni_hbm, w_no_hbm, w_cei_hbm, w_ceo_hbm, w_cni_hbm, w_cno_hbm,
    )
    targets = (
        nodes, group, halo, psend, precv, neigh, cneigh,
        w_ei, edges, w_eo, w_ni, w_no, w_cei, w_ceo, w_cni, w_cno,
    )
    for i, (source, target) in enumerate(zip(sources, targets)):
        copy = pltpu.make_async_copy(source, target, load_sems.at[i])
        copy.start()
        loads.append(copy)

    for i in range(3):
        loads[i].wait()
    own = nodes[...]
    own_halves = halves(own)
    group_pick = row_picker(spread_column(group[...], HIDDEN * 16, 4))
    group_src[...] = dot(group_pick, own_halves).astype(BF16).reshape(HIDDEN, 16, 128)
    ghost_pick = row_picker(spread_column(halo[0], MSG, 3))
    ghost_src[...] = dot(ghost_pick, own_halves).reshape(NODES, 8, 128)[:, :4].astype(BF16)

    pl.semaphore_wait(barrier, NODES - 1 + HIDDEN - 1)

    def low_first(visit):
        def step(z, carry):
            for dx in (2, 1, 3):
                visit(lax.rem(x_at + dx, NX) * NZ + z)

            @pl.when(z != z_at)
            def _():
                visit(x_at * NZ + z)

            return carry

        lax.fori_loop(0, NZ, step, 0, unroll=4)

    def send(src, dst, which, order=far_first):
        def visit(p):
            pltpu.make_async_remote_copy(
                src_ref=src.at[p],
                dst_ref=dst.at[node_at],
                send_sem=send_sems.at[which],
                recv_sem=recv_sems.at[which],
                device_id={"nodes": p},
                device_id_type=MESH,
            ).start()

        order(visit)

    def send_group(p):
        pltpu.make_async_remote_copy(
            src_ref=group_src.at[p],
            dst_ref=group_dst.at[hidden_at],
            send_sem=send_sems.at[0],
            recv_sem=recv_sems.at[0],
            device_id={"hidden": p},
            device_id_type=MESH,
        ).start()

    def wait_all(buffer, count, sem):
        pltpu.make_async_copy(buffer.at[pl.ds(0, count)], buffer.at[pl.ds(0, count)], sem).wait()

    group_first(send_group)
    send(ghost_src, ghost_dst, 1)

    for i in range(3, 7):
        loads[i].wait()
    lists = jnp.concatenate(
        [neigh[...].astype(F32), jnp.zeros((ROWS - SLOTS, ROWS), F32)], axis=0
    )
    neigh_columns = lists.T.astype(jnp.int32)
    column = jnp.concatenate([neigh_columns[:, k : k + 1] for k in range(SLOTS)], axis=0)
    lane = iota((EDGES, ROWS), 1)
    take_own = one_hot(column == lane)
    take_group = one_hot(column == lane + ROWS)
    take_ghost = one_hot(column == lane + 2 * ROWS)
    valid = column >= 0

    send_column = spread_column(psend[0], MSG, 3)
    send_row = spread_row(psend[0], MSG, 3)
    pool_pick = row_picker(send_column)
    shape = (2 * ROWS, MSG)
    sub = iota(shape, 0)
    back_pick = one_hot((send_row == (sub & 127)) & ((iota(shape, 1) & 1) == (sub >> 7)))
    recv_column = spread_column(precv[0], MSG, 3)
    recv_row = spread_row(precv[0], MSG, 3)
    shape = (2 * COARSE, MSG)
    sub = iota(shape, 0)
    member = one_hot((recv_row == (sub & 15)) & ((iota(shape, 1) & 1) == (sub >> 4)))
    shape = (MSG, 2 * COARSE)
    lane = iota(shape, 1)
    member_back = one_hot((recv_column == (lane & 15)) & ((iota(shape, 0) & 1) == (lane >> 4)))
    counts = jnp.sum(member[:COARSE].astype(F32), axis=1, keepdims=True)
    scale_down = jnp.maximum(counts, 1.0)

    lists = jnp.concatenate(
        [cneigh[...].astype(F32), jnp.zeros((8 - SLOTS, COARSE), F32)], axis=0
    )
    lists = jnp.concatenate([lists, jnp.zeros((8, 128 - COARSE), F32)], axis=1)
    lists = jnp.concatenate([lists, jnp.zeros((120, 128), F32)], axis=0)
    coarse_columns = lists.T[:COARSE].astype(jnp.int32)
    coarse_column = jnp.concatenate(
        [coarse_columns[:, k : k + 1] for k in range(SLOTS)], axis=0
    )
    take_coarse = one_hot(coarse_column == iota((COARSE_EDGES, COARSE), 1))
    coarse_valid = coarse_column >= 0

    def half_of(shape, half, shift, slot_bits):
        row = iota(shape, 0)
        lane = iota(shape, 1)
        wanted = ((row >> slot_bits) << shift) + ((row & ((1 << slot_bits) - 1)) << 1) + half
        return one_hot(lane == wanted)

    group_split = [half_of((ROWS, HIDDEN * 16), half, 4, 3) for half in range(2)]
    ghost_split = [half_of((ROWS, MSG), half, 3, 1) for half in range(2)]

    loads[7].wait()
    loads[8].wait()
    from_target = dot(own, w_ei[2 * WIDTH :, :])
    for k in range(SLOTS):
        rows = pl.ds(k * ROWS, ROWS)
        first_part[rows, :] = dot(edges[rows, :], w_ei[:WIDTH, :]) + from_target
    for i in range(9, 16):
        loads[i].wait()
    node_part = dot(own, w_ni[:WIDTH, :])
    from_own = dot(take_own, own)

    ghost_dst[pl.ds(node_at, 1)] = ghost_src[pl.ds(node_at, 1)]
    wait_all(ghost_dst, NODES - 1, recv_sems.at[1])

    def flat(buffer):
        return buffer[...].astype(F32).reshape(MSG, 128).astype(BF16)

    arrived = ghost_dst[...].astype(F32)
    arrived = jnp.concatenate([arrived, jnp.zeros_like(arrived)], axis=1)
    arrived = arrived.reshape(MSG, 128).astype(BF16)
    ghosts = jnp.concatenate([dot(split, arrived) for split in ghost_split], axis=1).astype(BF16)
    from_far = from_own + dot(take_ghost, ghosts)
    group_dst[pl.ds(hidden_at, 1)] = group_src[pl.ds(hidden_at, 1)]
    wait_all(group_dst, HIDDEN - 1, recv_sems.at[0])
    arrived = group_dst[...].reshape(HIDDEN * 16, 128)
    in_group = jnp.concatenate([dot(split, arrived) for split in group_split], axis=1).astype(BF16)
    source = (from_far + dot(take_group, in_group)).astype(BF16)

    total = None
    for c in range(0, UNITS, WIDTH):
        hidden = first_part[:, c : c + WIDTH] + dot(source, w_ei[WIDTH : 2 * WIDTH, c : c + WIDTH])
        part = dot(jnp.maximum(hidden, 0.0).astype(BF16), w_eo[c : c + WIDTH, :])
        total = part if total is None else total + part
    result = jnp.where(valid, edges[...].astype(F32) + layer_norm(total), 0.0).astype(BF16)
    edge_out[...] = result
    incoming = None
    for k in range(SLOTS):
        part = result[k * ROWS : (k + 1) * ROWS].astype(F32)
        incoming = part if incoming is None else incoming + part
    incoming = incoming.astype(BF16)
    hidden = jnp.maximum(node_part + dot(incoming, w_ni[WIDTH:, :]), 0.0).astype(BF16)
    fine_mid = (own.astype(F32) + layer_norm(dot(hidden, w_no[...]))).astype(BF16)

    pool_src[...] = dot(pool_pick, halves(fine_mid)).reshape(NODES, 8, 128).astype(BF16)
    send(pool_src, pool_dst, 2)
    pool_dst[pl.ds(node_at, 1)] = pool_src[pl.ds(node_at, 1)]
    wait_all(pool_dst, NODES - 1, recv_sems.at[2])

    sums = dot(member, flat(pool_dst))
    pooled = jnp.concatenate([sums[:COARSE], sums[COARSE:]], axis=1) / scale_down
    pooled = pooled.astype(BF16)
    from_target = dot(pooled, w_cei[WIDTH:, :])
    source = dot(take_coarse, pooled).astype(BF16)
    hidden = dot(source, w_cei[:WIDTH, :]) + jnp.concatenate([from_target] * SLOTS, axis=0)
    hidden = jnp.maximum(hidden, 0.0).astype(BF16)
    messages = jnp.where(coarse_valid, layer_norm(dot(hidden, w_ceo[...])), 0.0).astype(BF16)
    incoming = None
    for k in range(SLOTS):
        part = messages[k * COARSE : (k + 1) * COARSE].astype(F32)
        incoming = part if incoming is None else incoming + part
    incoming = incoming.astype(BF16)
    hidden = dot(pooled, w_cni[:WIDTH, :]) + dot(incoming, w_cni[WIDTH:, :])
    hidden = jnp.maximum(hidden, 0.0).astype(BF16)
    coarse = (pooled.astype(F32) + layer_norm(dot(hidden, w_cno[...]))).astype(BF16)
    coarse_out[...] = coarse

    back_src[...] = dot(member_back, halves(coarse)).reshape(NODES, 8, 128).astype(BF16)
    send(back_src, back_dst, 3, low_first)
    back_dst[pl.ds(node_at, 1)] = back_src[pl.ds(node_at, 1)]
    wait_all(back_dst, NODES - 1, recv_sems.at[3])

    returned = dot(back_pick, flat(back_dst))
    unpooled = jnp.concatenate([returned[:ROWS], returned[ROWS:]], axis=1)
    fine_out[...] = (fine_mid.astype(F32) + unpooled).astype(BF16)

    wait_all(group_dst, HIDDEN - 1, send_sems.at[0])
    for which, buffer in ((1, ghost_dst), (2, pool_dst), (3, back_dst)):
        wait_all(buffer, NODES - 1, send_sems.at[which])


def hand_over(*refs):
    sems = refs[-1]
    copies = [pltpu.make_async_copy(refs[i], refs[3 + i], sems.at[i]) for i in (0, 2)]
    for k in range(SLOTS):
        rows = pl.ds(k * ROWS, ROWS)
        copies.append(
            pltpu.make_async_copy(refs[1].at[rows], refs[4].at[rows], sems.at[3 + k])
        )
    for copy in copies:
        copy.start()
    for copy in copies:
        copy.wait()


def shards(
    fine_nodes, fine_edges, fine_neighbours, group_send, halo_send, pool_send, pool_recv,
    coarse_neighbours, *weights,
):
    anywhere = pl.BlockSpec(memory_space=pl.ANY)
    in_vmem = pl.BlockSpec(memory_space=pltpu.VMEM)
    operands = (
        fine_nodes,
        fine_edges.transpose(1, 0, 2).reshape(EDGES, WIDTH),
        fine_neighbours.T,
        group_send.transpose(0, 1, 3, 2),
        halo_send.transpose(0, 2, 1),
        pool_send.transpose(0, 2, 1),
        pool_recv.transpose(0, 2, 1),
        coarse_neighbours.T,
    ) + weights
    message = pltpu.VMEM((NODES, 8, 128), BF16)
    group_message = pltpu.VMEM((HIDDEN, 16, 128), BF16)
    results = (
        jax.ShapeDtypeStruct((ROWS, WIDTH), BF16),
        jax.ShapeDtypeStruct((EDGES, WIDTH), BF16),
        jax.ShapeDtypeStruct((COARSE, WIDTH), BF16),
    )
    held = pl.pallas_call(
        kernel,
        out_shape=tuple(pltpu.VMEM(r.shape, BF16) for r in results),
        in_specs=[anywhere] * len(operands),
        out_specs=(in_vmem,) * 3,
        scratch_shapes=[
            pltpu.VMEM((ROWS, WIDTH), BF16),
            pltpu.VMEM((EDGES, WIDTH), BF16),
            pltpu.VMEM((SLOTS, ROWS), jnp.int32),
            pltpu.VMEM((8, HIDDEN), jnp.int32),
            pltpu.VMEM((1, 2, NODES), jnp.int32),
            pltpu.VMEM((1, 4, NODES), jnp.int32),
            pltpu.VMEM((1, 4, NODES), jnp.int32),
            pltpu.VMEM((SLOTS, COARSE), jnp.int32),
        ]
        + [pltpu.VMEM(w.shape, BF16) for w in weights]
        + [
            pltpu.VMEM((EDGES, UNITS), F32),
            group_message, group_message,
            pltpu.VMEM((NODES, 4, 128), BF16), pltpu.VMEM((NODES, 4, 128), BF16),
            message, message, message, message,
            pltpu.SemaphoreType.DMA((16,)),
            pltpu.SemaphoreType.DMA((4,)),
            pltpu.SemaphoreType.DMA((4,)),
        ],
        compiler_params=pltpu.CompilerParams(
            collective_id=0, has_side_effects=True, vmem_limit_bytes=56 * 1024 * 1024
        ),
        cost_estimate=pl.CostEstimate(
            flops=2_100_000_000, bytes_accessed=8_000_000, transcendentals=2000
        ),
    )(*operands)
    fine_result, edge_result, coarse_result = pl.pallas_call(
        hand_over,
        out_shape=results,
        in_specs=[in_vmem] * 3,
        out_specs=(pl.BlockSpec(memory_space=pltpu.HBM),) * 3,
        scratch_shapes=[pltpu.SemaphoreType.DMA((3 + SLOTS,))],
        compiler_params=pltpu.CompilerParams(vmem_limit_bytes=56 * 1024 * 1024),
    )(*[pltpu.with_memory_space_constraint(h, pltpu.VMEM) for h in held])
    edge_result = edge_result.reshape(SLOTS, ROWS, WIDTH).transpose(1, 0, 2)
    return fine_result, edge_result, coarse_result


def solution(mesh):
    rows = ("nodes", "hidden")
    in_specs = (
        P(rows, None),
        P(rows, None, None),
        P(rows, None),
        P("nodes", None, None, None),
        P(rows, None, None),
        P(rows, None, None),
        P(rows, None, None),
        P(rows, None),
    ) + (P(),) * 8
    out_specs = (P(rows, None), P(rows, None, None), P(rows, None))
    return jax.shard_map(shards, mesh=mesh, in_specs=in_specs, out_specs=out_specs, check_vma=False)
```
